32 devices in a mesh: wide: 8 (over y, x, core), narrow: 4 (over z).
Axes of the slice: x: 2, y: 2, z: 4, core: 2. Of those that a mesh axis runs over, the one named last changes fastest.
Arguments:
- blocks: bfloat16 [8, 4, 16, 64, 4096], P('wide', 'narrow'), may hold values from -16 to 16
- row_tile: int32 [8, 4, 16], P('wide', 'narrow'), may hold values from 0 to 7
- col_tile: int32 [8, 4, 16], P('wide', 'narrow'), may hold values from 0 to 15, as said below
- depth_tile: int32 [8, 4, 16], P('wide', 'narrow'), may hold values from 0 to 15
- block_count: int32 [8, 4], P('wide', 'narrow'), may hold values from 4 to 16, as said below
- factor_b: bfloat16 [4096, 256], P(('wide', 'narrow')), may hold values from -40 to 40
- factor_c: bfloat16 [1024, 256], replicated, may hold values from -0.61035156 to 0.61035156
Outputs:
- a_new: float32 [4096, 256], P(('wide', 'narrow'))
- b_new: float32 [4096, 256], P(('wide', 'narrow'))
The draws below stay inside these ranges and needn't reach their ends.
Inputs may be any that keep to these rules, and one draw needn't show every extreme that they name: `block_count`: every device holds at least 4 live blocks, and some device exactly 16. col_tile // 2 is the index of wide that holds the block's mode-2 factor rows; among the 16 slots of one device, live or not, each such index appears at most 2 times, and some index exactly 2 times.
All inputs are finite; a program needn't handle non-finite values.
Results may differ from the reference program's by a relative error of at most 0.02.
Values may be sent and summed in bfloat16 or wider, within the bound.
A program may use at most 128 MiB of HBM per device.

```python
import jax
import jax.numpy as jnp
from jax import lax

R = 256
BS = 64
TI_DEV = 2
TJ_DEV = 2
NTK = 16
CAP = 16
SLOTS = 2
NI = 4096
NJ = 4096
N_WIDE = 8
N_NARROW = 4


def draw_blocks(key, part):
    key_core, key_scale = jax.random.split(key)
    shape = (N_WIDE, N_NARROW, CAP, BS, BS * BS)
    wide_pos = jnp.arange(N_WIDE, dtype=jnp.float32) / max(N_WIDE - 1, 1)
    trend = (2.0 * jnp.exp(jnp.log(12.0) * (wide_pos - 1.0))).reshape(N_WIDE, 1, 1, 1, 1)
    scale_draw = jax.random.uniform(key_scale, (N_WIDE, N_NARROW, CAP, 1, 1), jnp.float32)
    core = jnp.clip(jax.random.normal(key_core, shape, jnp.float32), -6.0, 6.0)
    block_scale = jnp.exp(jnp.log(3.0) * (scale_draw - 0.5))
    return jnp.clip(core * trend * block_scale, -16.0, 16.0).astype(jnp.bfloat16)


def draw_block_count(key, part):
    key_base, key_full = jax.random.split(key)
    total_devices = N_WIDE * N_NARROW
    low_count = max(1, CAP // 4)
    high_count = max(low_count + 1, CAP)
    base_counts = jax.random.randint(key_base, (total_devices,), low_count, high_count, dtype=jnp.int32)
    fuller = jax.random.randint(key_full, (), 0, total_devices, dtype=jnp.int32)
    counts = jnp.where(jnp.arange(total_devices, dtype=jnp.int32) == fuller, CAP, base_counts)
    return counts.reshape(N_WIDE, N_NARROW).astype(jnp.int32)


def draw_col_tile(key, part):
    key_perm, key_local = jax.random.split(key)
    total_devices = N_WIDE * N_NARROW
    device_keys = jax.random.split(key_perm, total_devices)
    picks = jax.vmap(lambda one_key: jax.random.permutation(one_key, N_WIDE * SLOTS)[:CAP])(device_keys)
    owners = picks.astype(jnp.int32) % N_WIDE
    inside = jax.random.randint(key_local, (total_devices, CAP), 0, TJ_DEV, dtype=jnp.int32)
    return (owners * TJ_DEV + inside).reshape(N_WIDE, N_NARROW, CAP).astype(jnp.int32)


def pair_plan(key):
    plan_key = jax.random.fold_in(key, 4099)
    key_perm, key_depth = jax.random.split(plan_key)
    column_order = jax.random.permutation(key_perm, R).astype(jnp.int32)
    positions = jnp.arange(R, dtype=jnp.int32)
    partner = jnp.zeros((R,), jnp.int32).at[column_order].set(column_order[jnp.bitwise_xor(positions, 1)])
    leader = jnp.zeros((R,), jnp.int32).at[column_order].set(1 - positions % 2)
    pair_id = jnp.zeros((R,), jnp.int32).at[column_order].set(positions // 2)
    depth_draw = jax.random.uniform(key_depth, (R // 2,), jnp.float32)
    residue = jnp.exp(jnp.log(0.002) * depth_draw)
    return (partner, leader, jnp.take(residue, pair_id), pair_id)


def factor_body(key, rows, bound, plan, boost):
    key_core, key_shift, key_spread, key_column = jax.random.split(key, 4)
    position = jnp.arange(rows, dtype=jnp.float32) / rows
    trend = (0.5 * (1.0 + 2.0 * position)).reshape(rows, 1)
    spread_draw = jax.random.uniform(key_spread, (rows, 1), jnp.float32)
    column_draw = jax.random.uniform(key_column, (1, R), jnp.float32)
    core = jnp.clip(jax.random.normal(key_core, (rows, R), jnp.float32), -6.0, 6.0)
    column_shift = jax.random.uniform(key_shift, (1, R), jnp.float32, -0.6, 0.6)
    spread = jnp.exp(jnp.log(10.0) * (spread_draw - 0.5))
    column_scale = jnp.exp(bound * (column_draw - 0.5))
    values = (core + column_shift) * spread * trend * boost
    partner, leader, residue, pair_id = plan
    partner_values = jnp.take(values, partner, axis=1)
    follower = jnp.sqrt(1.0 - residue)[None, :] * partner_values + jnp.sqrt(residue)[None, :] * values
    mixed = jnp.where(leader[None, :] > 0, values, follower)
    return (mixed, column_scale)


def draw_factor_b(key, part):
    rows = TJ_DEV * N_WIDE * N_NARROW * BS
    total_devices = N_WIDE * N_NARROW
    plan = pair_plan(key)
    pair_id = plan[3]
    half_rank = R // 2
    pair_order = jax.random.permutation(jax.random.fold_in(key, 21), half_rank).astype(jnp.int32)
    device_ids = jnp.arange(total_devices, dtype=jnp.int32)
    heavy_pair = jnp.take(pair_order, device_ids % half_rank)
    boosted = (device_ids // half_rank % 4 == 0).astype(jnp.float32)
    hit = (heavy_pair[:, None] == pair_id[None, :]).astype(jnp.float32)
    boost_dev = 1.0 + 7.0 * hit * boosted[:, None]
    boost = jnp.repeat(boost_dev, TJ_DEV * BS, axis=0)
    values, column_scale = factor_body(jax.random.fold_in(key, 11), rows, 0.0, plan, boost)
    return jnp.clip(values, -40.0, 40.0).astype(jnp.bfloat16)


def draw_factor_c(key, part):
    rows = NTK * BS
    gamma = 1.0 / (TJ_DEV * N_WIDE * N_NARROW * NTK * BS)
    plan = pair_plan(key)
    lift = (1.0 / plan[2]).reshape(1, R)
    values, column_scale = factor_body(jax.random.fold_in(key, 12), rows, jnp.log(4.0), plan, 1.0)
    return (jnp.clip(values * column_scale * lift, -40000.0, 40000.0) * gamma).astype(jnp.bfloat16)


def plant(result, key, low, high):
    place = [jax.random.randint(jax.random.fold_in(key, axis), (), 0, length) for axis, length in enumerate(result.shape)]
    widest = result.shape.index(max(result.shape))
    beside = place[:widest] + [(place[widest] + 1) % result.shape[widest]] + place[widest + 1:]
    return result.at[tuple(place)].set(low).at[tuple(beside)].set(high)


def setup_inputs(seed: int = 0) -> dict:
    splits = jax.random.split(jax.random.key(seed), 8)
    return {
        "blocks": draw_blocks(jax.random.fold_in(splits[7], 71), 0),
        "row_tile": plant(jax.random.randint(splits[1], (N_WIDE, N_NARROW, CAP), 0, N_NARROW * TI_DEV), jax.random.fold_in(splits[1], 1), 0, (N_NARROW * TI_DEV) - 1).astype(jnp.int32),
        "col_tile": draw_col_tile(jax.random.fold_in(splits[7], 71), 0),
        "depth_tile": plant(jax.random.randint(splits[3], (N_WIDE, N_NARROW, CAP), 0, NTK), jax.random.fold_in(splits[3], 1), 0, NTK - 1).astype(jnp.int32),
        "block_count": draw_block_count(jax.random.fold_in(splits[7], 71), 0),
        "factor_b": draw_factor_b(jax.random.fold_in(splits[7], 71), 0),
        "factor_c": draw_factor_c(jax.random.fold_in(splits[7], 71), 0),
    }


def right_solve(target, matrix):
    chol_lower = jnp.linalg.cholesky(matrix)
    middle = lax.linalg.triangular_solve(chol_lower, target, left_side=False, lower=True, transpose_a=True)
    return lax.linalg.triangular_solve(chol_lower, middle, left_side=False, lower=True, transpose_a=False)

def depth_mix(one_block, depth_id, factor_c):
    depth_rows = lax.dynamic_slice_in_dim(factor_c, depth_id * BS, BS, 0)
    depth_mixed = lax.dot_general(one_block.astype(jnp.float32), depth_rows.astype(jnp.float32), (((0,), (0,)), ((), ())), preferred_element_type=jnp.float32)
    return depth_mixed.reshape(BS, BS, depth_rows.shape[1])

def flatten(values):
    return values.reshape(-1).astype(jnp.int32)

def reference(blocks, row_tile, col_tile, depth_tile, block_count, factor_b, factor_c):
    rank_width = factor_c.shape[1]
    slot_ids = jnp.arange(CAP, dtype=jnp.int32)
    wide_ids = jnp.arange(N_WIDE, dtype=jnp.int32)[:, None, None]
    narrow_ids = jnp.arange(N_NARROW, dtype=jnp.int32)[None, :, None]
    alive_mask = (slot_ids[None, None, :] < block_count[:, :, None]).astype(jnp.int32)
    first_tile = wide_ids * (N_NARROW * TI_DEV) + row_tile
    owners = col_tile // TJ_DEV
    second_tile = (owners * N_NARROW + narrow_ids) * TJ_DEV + col_tile % TJ_DEV
    scan_items = (blocks.reshape(-1, BS, BS * BS), flatten(first_tile), flatten(second_tile), flatten(depth_tile), flatten(alive_mask))
    gram_c = jnp.dot(factor_c.T.astype(jnp.float32), factor_c.astype(jnp.float32), preferred_element_type=jnp.float32)
    gram_b = jnp.dot(factor_b.T.astype(jnp.float32), factor_b.astype(jnp.float32), preferred_element_type=jnp.float32)

    def first_pass(partial_sum, item):
        one_block, first_id, second_id, depth_id, alive = item

        def add_block(running):
            depth_mixed = depth_mix(one_block, depth_id, factor_c)
            b_rows = lax.dynamic_slice_in_dim(factor_b, second_id * BS, BS, 0).astype(jnp.float32)
            b_term = jnp.sum(depth_mixed * b_rows[None, :, :], axis=1)
            current = lax.dynamic_slice_in_dim(running, first_id * BS, BS, 0)
            return lax.dynamic_update_slice_in_dim(running, current + b_term, first_id * BS, 0)
        return (lax.cond(alive > 0, add_block, lambda running: running, partial_sum), None)
    mttkrp_a, _ = lax.scan(first_pass, jnp.zeros((NI, rank_width), jnp.float32), scan_items)
    a_new = right_solve(mttkrp_a, gram_b * gram_c)
    a_half = a_new.astype(jnp.bfloat16)
    gram_a = jnp.dot(a_half.T.astype(jnp.float32), a_half.astype(jnp.float32), preferred_element_type=jnp.float32)

    def second_pass(partial_sum, item):
        one_block, first_id, second_id, depth_id, alive = item

        def add_block(running):
            depth_mixed = depth_mix(one_block, depth_id, factor_c)
            a_part = lax.dynamic_slice_in_dim(a_half, first_id * BS, BS, 0).astype(jnp.float32)
            a_term = jnp.sum(depth_mixed * a_part[:, None, :], axis=0)
            current = lax.dynamic_slice_in_dim(running, second_id * BS, BS, 0)
            return lax.dynamic_update_slice_in_dim(running, current + a_term, second_id * BS, 0)
        return (lax.cond(alive > 0, add_block, lambda running: running, partial_sum), None)
    mttkrp_b, _ = lax.scan(second_pass, jnp.zeros((NJ, rank_width), jnp.float32), scan_items)
    b_new = right_solve(mttkrp_b, gram_a * gram_c)
    return (a_new, b_new)
```

```python
import functools

import jax
import jax.numpy as jnp
from jax import lax
from jax.experimental import pallas as pl
from jax.experimental.pallas import tpu as pltpu
from jax.sharding import PartitionSpec as P

VMEM = pl.BlockSpec(memory_space=pltpu.VMEM)
HIGH = lax.Precision.HIGHEST
NB = 64


def dot(x, y, x_dim, y_dim, precision=None):
    return lax.dot_general(
        x, y, (((x_dim,), (y_dim,)), ((), ())), precision=precision,
        preferred_element_type=jnp.float32,
    )


def pass_kernel(first, rows, load_id, store_id, depth_id, count, x_ref, c_ref, f_ref, out_ref):
    slot = pl.program_id(0)

    @pl.when(slot == 0)
    def _():
        out_ref[...] = jnp.zeros_like(out_ref)

    @pl.when(slot < count[0])
    def _():
        depth_rows = c_ref[pl.ds(pl.multiple_of(depth_id[slot] * rows, rows), rows), :]
        tile = f_ref[pl.ds(pl.multiple_of(load_id[slot] * rows, rows), rows), :].astype(jnp.float32)
        target = pl.multiple_of(store_id[slot] * rows, rows)
        step = 8
        total = None
        for a in range(0, rows, step):
            x = x_ref[0, :, a * rows : (a + step) * rows]
            mix = dot(x, depth_rows, 0, 0).reshape(step, rows, -1)
            if first:
                at = pl.ds(target + a, step)
                out_ref[at, :] += jnp.sum(mix * tile[None], axis=1)
            else:
                term = jnp.sum(mix * tile[a : a + step][:, None, :], axis=0)
                total = term if total is None else total + term
        if not first:
            out_ref[pl.ds(target, rows), :] += total


def mix_pass(first, x, load_id, store_id, depth_id, count, c, f, out_rows):
    cap, rows, width = x.shape
    rank = c.shape[1]
    whole = lambda a: pl.BlockSpec(a.shape, lambda s, *_: (0, 0))
    return pl.pallas_call(
        functools.partial(pass_kernel, first, rows),
        out_shape=jax.ShapeDtypeStruct((out_rows, rank), jnp.float32),
        grid_spec=pltpu.PrefetchScalarGridSpec(
            num_scalar_prefetch=4,
            grid=(cap,),
            in_specs=[
                pl.BlockSpec(
                    (1, rows, width),
                    lambda s, l, t, d, n: (jnp.minimum(s, n[0] - 1), 0, 0),
                ),
                whole(c),
                whole(f),
            ],
            out_specs=pl.BlockSpec((out_rows, rank), lambda s, *_: (0, 0)),
        ),
        cost_estimate=pl.CostEstimate(
            flops=cap * rows * width * rank * 8, bytes_accessed=x.size * 2, transcendentals=0
        ),
        compiler_params=pltpu.CompilerParams(vmem_limit_bytes=40 * 1024 * 1024),
    )(load_id, store_id, depth_id, count, x, c, f)


def root_kernel(gram_ref, c_ref, w_ref, work):
    rank = gram_ref.shape[0]
    c = c_ref[...]
    work[:, :rank] = gram_ref[...] * dot(c, c, 0, 0)
    row_id = lax.broadcasted_iota(jnp.int32, (rank, rank), 0)
    col_id = lax.broadcasted_iota(jnp.int32, (rank, rank), 1)
    work[:, rank:] = (row_id == col_id).astype(jnp.float32)
    row = lax.broadcasted_iota(jnp.int32, (NB, 2 * NB), 0)
    lane = lax.broadcasted_iota(jnp.int32, (NB, 2 * NB), 1)
    wide_lane = lax.broadcasted_iota(jnp.int32, (NB, rank), 1)

    def block_step(k, carry):
        at = pl.ds(pl.multiple_of(k * NB, NB), NB)
        tile = work[at, pl.ds(pl.multiple_of(k // 2 * 2 * NB, 2 * NB), 2 * NB)]
        tile = jnp.where(k % 2 == 1, pltpu.roll(tile, NB, 1), tile)
        parts = jnp.where(lane < NB, tile, (lane - NB == row).astype(jnp.float32))
        parts = [parts[i : i + 8] for i in range(0, NB, 8)]
        sub = row[:8]
        for j in range(NB):
            top = j // 8
            cols = [jnp.broadcast_to(parts[i][:, j : j + 1], (8, 2 * NB)) for i in range(top, NB // 8)]
            pivot_row = parts[top][j % 8 : j % 8 + 1, :]
            scaled = pivot_row / cols[0][j % 8 : j % 8 + 1, :]
            for i in range(top, NB // 8):
                factor = cols[i - top]
                if i == top:
                    factor = jnp.where(sub > j % 8, factor, 0.0)
                parts[i] = parts[i] - factor * scaled
        done = jnp.concatenate(parts, axis=0)
        diag = jnp.sum(jnp.where(lane == row, done, 0.0), axis=1, keepdims=True)
        root = done * lax.rsqrt(diag)
        head = dot(root[:, NB:], work[at, :], 1, 0, HIGH)
        w_ref[at, :] = head[:, rank:]
        below = jnp.where(wide_lane >= (k + 1) * NB, head[:, :rank], 0.0)
        work[...] = work[...] - dot(below, head, 0, 0, HIGH)
        return carry

    lax.fori_loop(0, rank // NB, block_step, 0)


def inverse_root(gram, c):
    rank = gram.shape[0]
    return pl.pallas_call(
        root_kernel,
        out_shape=jax.ShapeDtypeStruct((rank, rank), jnp.float32),
        in_specs=[VMEM] * 2,
        out_specs=VMEM,
        scratch_shapes=[pltpu.VMEM((rank, 2 * rank), jnp.float32)],
        cost_estimate=pl.CostEstimate(flops=10**9, bytes_accessed=10**6, transcendentals=0),
        compiler_params=pltpu.CompilerParams(vmem_limit_bytes=40 * 1024 * 1024),
    )(gram, c)


def apply_kernel(m_ref, w_ref, new_ref, *rest):
    w = w_ref[...]
    new = dot(dot(m_ref[...], w, 1, 1, HIGH), w, 1, 0, HIGH)
    new_ref[...] = new
    if rest:
        half = new.astype(jnp.bfloat16)
        rest[0][...] = half
        rest[1][...] = dot(half, half, 0, 0)


def apply_root(m, w, more):
    rank = w.shape[0]
    out_shape = [jax.ShapeDtypeStruct(m.shape, jnp.float32)]
    if more:
        out_shape += [
            jax.ShapeDtypeStruct(m.shape, jnp.bfloat16),
            jax.ShapeDtypeStruct((rank, rank), jnp.float32),
        ]
    return pl.pallas_call(
        apply_kernel,
        out_shape=out_shape,
        in_specs=[VMEM] * 2,
        out_specs=[VMEM] * len(out_shape),
        compiler_params=pltpu.CompilerParams(vmem_limit_bytes=40 * 1024 * 1024),
    )(m, w)


def local(blocks, row_tile, col_tile, depth_tile, block_count, factor_b, factor_c):
    x = blocks[0, 0]
    first_ids = row_tile[0, 0]
    second_ids = col_tile[0, 0]
    depth_ids = depth_tile[0, 0]
    count = block_count[0]
    rows = x.shape[1]
    wide_count = lax.axis_size("wide")
    narrow_count = lax.axis_size("narrow")
    local_rows = factor_b.shape[0]

    gathered = lax.all_gather(factor_b, "wide", axis=0, tiled=True)
    gram_b = lax.psum(dot(factor_b, factor_b, 0, 0), ("wide", "narrow"))
    first_part = mix_pass(
        True, x, second_ids, first_ids, depth_ids, count, factor_c, gathered, narrow_count * local_rows
    )
    mttkrp_a = lax.psum_scatter(first_part, "narrow", scatter_dimension=0, tiled=True)
    root_a = inverse_root(gram_b, factor_c)
    a_new, a_half, gram_a = apply_root(mttkrp_a, root_a, True)
    a_rows = lax.all_gather(a_half, "narrow", axis=0, tiled=True)
    gram_a = lax.psum(gram_a, ("wide", "narrow"))
    second_part = mix_pass(
        False, x, first_ids, second_ids, depth_ids, count, factor_c, a_rows, wide_count * local_rows
    )
    mttkrp_b = lax.psum_scatter(second_part, "wide", scatter_dimension=0, tiled=True)
    root_b = inverse_root(gram_a, factor_c)
    (b_new,) = apply_root(mttkrp_b, root_b, False)
    return (a_new, b_new)


def solution(mesh):
    return jax.shard_map(
        local,
        mesh=mesh,
        in_specs=(
            P("wide", "narrow", None, None, None),
            P("wide", "narrow", None),
            P("wide", "narrow", None),
            P("wide", "narrow", None),
            P("wide", "narrow"),
            P(("wide", "narrow"), None),
            P(),
        ),
        out_specs=(P(("wide", "narrow"), None), P(("wide", "narrow"), None)),
        check_vma=False,
    )
```

```python
import functools

import jax
import jax.numpy as jnp
from jax import lax
from jax.experimental import pallas as pl
from jax.experimental.pallas import tpu as pltpu
from jax.sharding import PartitionSpec as P

VMEM = pl.BlockSpec(memory_space=pltpu.VMEM)
HIGH = lax.Precision.HIGHEST
NB = 64


def dot(x, y, x_dim, y_dim, precision=None):
    return lax.dot_general(
        x, y, (((x_dim,), (y_dim,)), ((), ())), precision=precision,
        preferred_element_type=jnp.float32,
    )


def pass_kernel(first, rows, load_id, store_id, depth_id, count, x_ref, c_ref, f_ref, out_ref):
    slot = pl.program_id(0)

    @pl.when(slot == 0)
    def _():
        out_ref[...] = jnp.zeros_like(out_ref)

    @pl.when(slot < count[0])
    def _():
        depth_rows = c_ref[pl.ds(pl.multiple_of(depth_id[slot] * rows, rows), rows), :]
        tile = f_ref[pl.ds(pl.multiple_of(load_id[slot] * rows, rows), rows), :].astype(jnp.float32)
        target = pl.multiple_of(store_id[slot] * rows, rows)
        step = 8
        total = None
        for a in range(0, rows, step):
            x = x_ref[0, :, a * rows : (a + step) * rows]
            mix = dot(x, depth_rows, 0, 0).reshape(step, rows, -1)
            if first:
                at = pl.ds(target + a, step)
                out_ref[at, :] += jnp.sum(mix * tile[None], axis=1)
            else:
                term = jnp.sum(mix * tile[a : a + step][:, None, :], axis=0)
                total = term if total is None else total + term
        if not first:
            out_ref[pl.ds(target, rows), :] += total


def mix_pass(first, x, load_id, store_id, depth_id, count, c, f, out_rows):
    cap, rows, width = x.shape
    rank = c.shape[1]
    whole = lambda a: pl.BlockSpec(a.shape, lambda s, *_: (0, 0))
    return pl.pallas_call(
        functools.partial(pass_kernel, first, rows),
        out_shape=jax.ShapeDtypeStruct((out_rows, rank), jnp.float32),
        grid_spec=pltpu.PrefetchScalarGridSpec(
            num_scalar_prefetch=4,
            grid=(cap,),
            in_specs=[
                pl.BlockSpec(
                    (1, rows, width),
                    lambda s, l, t, d, n: (jnp.minimum(s, n[0] - 1), 0, 0),
                ),
                whole(c),
                whole(f),
            ],
            out_specs=pl.BlockSpec((out_rows, rank), lambda s, *_: (0, 0)),
        ),
        cost_estimate=pl.CostEstimate(
            flops=cap * rows * width * rank * 8, bytes_accessed=x.size * 2, transcendentals=0
        ),
        compiler_params=pltpu.CompilerParams(vmem_limit_bytes=40 * 1024 * 1024),
    )(load_id, store_id, depth_id, count, x, c, f)


def root_steps(gram_ref, gram_c_ref, w_ref, work):
    rank = gram_ref.shape[0]
    pair = 2 * NB
    work[:, :rank] = gram_ref[...] * gram_c_ref[...]
    row_id = lax.broadcasted_iota(jnp.int32, (rank, rank), 0)
    col_id = lax.broadcasted_iota(jnp.int32, (rank, rank), 1)
    work[:, rank:] = (row_id == col_id).astype(jnp.float32)
    row = lax.broadcasted_iota(jnp.int32, (NB, pair), 0)
    lane = lax.broadcasted_iota(jnp.int32, (NB, pair), 1)
    sub = row[:8]

    for k in range(rank // NB):
        lo, hi = k * NB, (k + 1) * NB
        at = lo // pair * pair
        tile = work[lo:hi, at : at + pair]
        if lo != at:
            tile = pltpu.roll(tile, NB, 1)
        full = jnp.where(lane < NB, tile, (lane - NB == row).astype(jnp.float32))
        parts = [full[i : i + 8] for i in range(0, NB, 8)]
        for j in range(0, NB, 2):
            top, inner = j // 8, j % 8
            rest = range(top, NB // 8)
            first = {i: jnp.broadcast_to(parts[i][:, j : j + 1], (8, pair)) for i in rest}
            second = {i: jnp.broadcast_to(parts[i][:, j + 1 : j + 2], (8, pair)) for i in rest}
            row0 = parts[top][inner : inner + 1, :]
            row1 = parts[top][inner + 1 : inner + 2, :]
            p = first[top][inner : inner + 1, :]
            q = second[top][inner : inner + 1, :]
            r = second[top][inner + 1 : inner + 2, :]
            inverse = 1.0 / (p * r - q * q)
            scaled0 = (r * row0 - q * row1) * inverse
            scaled1 = (p * row1 - q * row0) * inverse
            for i in rest:
                if i == top and inner == 6:
                    continue
                term = first[i] * scaled0 + second[i] * scaled1
                if i == top:
                    term = jnp.where(sub > inner + 1, term, 0.0)
                parts[i] = parts[i] - term
        done = jnp.concatenate(parts, axis=0)
        above = pltpu.roll(done, 1, 0)
        odd = row % 2 == 1
        before = lane == row - 1
        p = jnp.sum(jnp.where(before, above, 0.0), axis=1, keepdims=True)
        q = jnp.sum(jnp.where(before, done, 0.0), axis=1, keepdims=True)
        ratio = q / jnp.where(odd, p, 1.0)
        done = jnp.where(odd, done - ratio * above, done)
        diag = jnp.sum(jnp.where(lane == row, done, 0.0), axis=1, keepdims=True)
        root = (done * lax.rsqrt(diag))[:, NB:]
        stop = rank + (hi + pair - 1) // pair * pair
        w_ref[lo:hi, :] = jnp.zeros((NB, rank), jnp.float32)
        tail = dot(root, work[lo:hi, rank:stop], 1, 0, HIGH)
        w_ref[lo:hi, : stop - rank] = tail
        if hi < rank:
            start = hi // pair * pair
            head = dot(root, work[lo:hi, start:rank], 1, 0, HIGH)
            work[start:rank, start:rank] -= dot(head, head, 0, 0, HIGH)
            work[hi:rank, rank:stop] -= dot(head, tail, 0, 0, HIGH)[hi - start :]


def inverse_root(gram, gram_c):
    rank = gram.shape[0]
    return pl.pallas_call(
        root_steps,
        out_shape=jax.ShapeDtypeStruct((rank, rank), jnp.float32),
        in_specs=[VMEM] * 2,
        out_specs=VMEM,
        scratch_shapes=[pltpu.VMEM((rank, 2 * rank), jnp.float32)],
        compiler_params=pltpu.CompilerParams(vmem_limit_bytes=40 * 1024 * 1024),
    )(gram, gram_c)


def greet(axes):
    barrier = pltpu.get_barrier_semaphore()
    total = 0
    for axis, n in axes.items():
        me = lax.axis_index(axis)
        for k in range(1, n):
            pl.semaphore_signal(
                barrier, inc=1, device_id={axis: lax.rem(me + k, n)}, device_id_type=pl.DeviceIdType.MESH
            )
        total += n - 1
    pl.semaphore_wait(barrier, total)


def exchange(axis, n, source, target, sems):
    me = lax.axis_index(axis)
    copies = []
    for k in range(1, n):
        peer = lax.rem(me + k, n)
        copy = pltpu.make_async_remote_copy(
            src_ref=source(peer),
            dst_ref=target,
            send_sem=sems.at[0, k - 1],
            recv_sem=sems.at[1, k - 1],
            device_id={axis: peer},
            device_id_type=pl.DeviceIdType.MESH,
        )
        copy.start()
        copies.append(copy)
    return copies


def finish(copies):
    for copy in copies:
        copy.wait()


def added(stage, n):
    total = stage[0]
    for i in range(1, n):
        total = total + stage[i]
    return total


def share(index, rows):
    return pl.ds(pl.multiple_of(index * rows, rows), rows)


def sum_all(wide, narrow, part, out, stage_w, stage_n, sems_w, sems_n, sems_g, beside=None):
    me_w, me_n = lax.axis_index("wide"), lax.axis_index("narrow")
    rows = part.shape[0] // wide
    mine = share(me_w, rows)
    copies = exchange("wide", wide, lambda peer: part.at[share(peer, rows)], stage_w.at[me_w], sems_w)
    stage_w[me_w] = part[mine, :]
    if beside is not None:
        beside()
    finish(copies)
    stage_n[me_n] = added(stage_w, wide)
    finish(exchange("narrow", narrow, lambda peer: stage_n.at[me_n], stage_n.at[me_n], sems_n))
    out[mine, :] = added(stage_n, narrow)
    finish(exchange("wide", wide, lambda peer: out.at[mine], out.at[mine], sems_g))


def sum_scratch(wide, narrow, rank):
    return [
        pltpu.VMEM((rank, rank), jnp.float32),
        pltpu.VMEM((wide, rank // wide, rank), jnp.float32),
        pltpu.VMEM((narrow, rank // wide, rank), jnp.float32),
        pltpu.SemaphoreType.DMA((2, wide)),
        pltpu.SemaphoreType.DMA((2, narrow)),
        pltpu.SemaphoreType.DMA((2, wide)),
    ]


def params(collective):
    return pltpu.CompilerParams(
        collective_id=collective, has_side_effects=True, vmem_limit_bytes=40 * 1024 * 1024
    )


def start_kernel(wide, narrow, b_ref, c_ref, rows_ref, gram_ref, gram_c_ref, part, *rest):
    *sum_rest, sems = rest
    me = lax.axis_index("wide")
    rows = b_ref.shape[0]
    greet({"wide": wide, "narrow": narrow})
    b = b_ref[...]
    part[...] = dot(b, b, 0, 0)
    mine = share(me, rows)

    def beside():
        rows_ref[mine, :] = b
        c = c_ref[...]
        gram_c_ref[...] = dot(c, c, 0, 0)

    copies = exchange("wide", wide, lambda peer: b_ref, rows_ref.at[mine], sems)
    sum_all(wide, narrow, part, gram_ref, *sum_rest, beside)
    finish(copies)


def start(wide, narrow, b, c):
    rows, rank = b.shape
    return pl.pallas_call(
        functools.partial(start_kernel, wide, narrow),
        out_shape=[
            jax.ShapeDtypeStruct((wide * rows, rank), b.dtype),
            jax.ShapeDtypeStruct((rank, rank), jnp.float32),
            jax.ShapeDtypeStruct((rank, rank), jnp.float32),
        ],
        in_specs=[VMEM] * 2,
        out_specs=[VMEM] * 3,
        scratch_shapes=sum_scratch(wide, narrow, rank) + [pltpu.SemaphoreType.DMA((2, wide))],
        compiler_params=params(0),
    )(b, c)


def middle_kernel(wide, narrow, sum_ref, w_ref, new_ref, rows_ref, gram_ref, part, *rest):
    *sum_rest, stage, sems, sems_a = rest
    me = lax.axis_index("narrow")
    rows = new_ref.shape[0]
    greet({"wide": wide, "narrow": narrow})
    mine = share(me, rows)
    copies = exchange("narrow", narrow, lambda peer: sum_ref.at[share(peer, rows)], stage.at[me], sems)
    stage[me] = sum_ref[mine, :]
    finish(copies)
    w = w_ref[...]
    new = dot(dot(added(stage, narrow), w, 1, 1, HIGH), w, 1, 0, HIGH)
    half = new.astype(jnp.bfloat16)
    rows_ref[mine, :] = half
    copies = exchange("narrow", narrow, lambda peer: rows_ref.at[mine], rows_ref.at[mine], sems_a)
    part[...] = dot(half, half, 0, 0)

    def beside():
        new_ref[...] = new

    sum_all(wide, narrow, part, gram_ref, *sum_rest, beside)
    finish(copies)


def middle(wide, narrow, first_part, w):
    rows, rank = first_part.shape[0] // narrow, first_part.shape[1]
    return pl.pallas_call(
        functools.partial(middle_kernel, wide, narrow),
        out_shape=[
            jax.ShapeDtypeStruct((rows, rank), jnp.float32),
            jax.ShapeDtypeStruct((narrow * rows, rank), jnp.bfloat16),
            jax.ShapeDtypeStruct((rank, rank), jnp.float32),
        ],
        in_specs=[VMEM] * 2,
        out_specs=[VMEM] * 3,
        scratch_shapes=sum_scratch(wide, narrow, rank)
        + [
            pltpu.VMEM((narrow, rows, rank), jnp.float32),
            pltpu.SemaphoreType.DMA((2, narrow)),
            pltpu.SemaphoreType.DMA((2, narrow)),
        ],
        compiler_params=params(1),
    )(first_part, w)


def last_kernel(wide, sum_ref, w_ref, new_ref, stage, sems):
    me = lax.axis_index("wide")
    rows = new_ref.shape[0]
    greet({"wide": wide})
    copies = exchange("wide", wide, lambda peer: sum_ref.at[share(peer, rows)], stage.at[me], sems)
    stage[me] = sum_ref[share(me, rows), :]
    finish(copies)
    w = w_ref[...]
    new_ref[...] = dot(dot(added(stage, wide), w, 1, 1, HIGH), w, 1, 0, HIGH)


def last(wide, second_part, w):
    rows, rank = second_part.shape[0] // wide, second_part.shape[1]
    return pl.pallas_call(
        functools.partial(last_kernel, wide),
        out_shape=jax.ShapeDtypeStruct((rows, rank), jnp.float32),
        in_specs=[VMEM] * 2,
        out_specs=VMEM,
        scratch_shapes=[
            pltpu.VMEM((wide, rows, rank), jnp.float32),
            pltpu.SemaphoreType.DMA((2, wide)),
        ],
        compiler_params=params(2),
    )(second_part, w)


def local(blocks, row_tile, col_tile, depth_tile, block_count, factor_b, factor_c):
    x = blocks[0, 0]
    first_ids = row_tile[0, 0]
    second_ids = col_tile[0, 0]
    depth_ids = depth_tile[0, 0]
    count = block_count[0]
    wide = lax.axis_size("wide")
    narrow = lax.axis_size("narrow")
    rows = factor_b.shape[0]

    b_rows, gram_b, gram_c = start(wide, narrow, factor_b, factor_c)
    first_part = mix_pass(
        True, x, second_ids, first_ids, depth_ids, count, factor_c, b_rows, narrow * rows
    )
    a_new, a_rows, gram_a = middle(wide, narrow, first_part, inverse_root(gram_b, gram_c))
    second_part = mix_pass(
        False, x, first_ids, second_ids, depth_ids, count, factor_c, a_rows, wide * rows
    )
    b_new = last(wide, second_part, inverse_root(gram_a, gram_c))
    return (a_new, b_new)


def solution(mesh):
    return jax.shard_map(
        local,
        mesh=mesh,
        in_specs=(
            P("wide", "narrow", None, None, None),
            P("wide", "narrow", None),
            P("wide", "narrow", None),
            P("wide", "narrow", None),
            P("wide", "narrow"),
            P(("wide", "narrow"), None),
            P(),
        ),
        out_specs=(P(("wide", "narrow"), None), P(("wide", "narrow"), None)),
        check_vma=False,
    )
```

```python
import functools

import jax
import jax.numpy as jnp
from jax import lax
from jax.experimental import pallas as pl
from jax.experimental.pallas import tpu as pltpu
from jax.sharding import PartitionSpec as P

VMEM = pl.BlockSpec(memory_space=pltpu.VMEM)
HIGH = lax.Precision.HIGHEST
NB = 64


def dot(x, y, x_dim, y_dim, precision=None):
    return lax.dot_general(
        x, y, (((x_dim,), (y_dim,)), ((), ())), precision=precision,
        preferred_element_type=jnp.float32,
    )


def pass_kernel(first, rows, load_id, store_id, depth_id, count, x_ref, c_ref, f_ref, out_ref):
    slot = pl.program_id(0)

    @pl.when(slot == 0)
    def _():
        out_ref[...] = jnp.zeros_like(out_ref)

    @pl.when(slot < count[0])
    def _():
        depth_rows = c_ref[pl.ds(pl.multiple_of(depth_id[slot] * rows, rows), rows), :]
        tile = f_ref[pl.ds(pl.multiple_of(load_id[slot] * rows, rows), rows), :].astype(jnp.float32)
        target = pl.multiple_of(store_id[slot] * rows, rows)
        step = 8
        total = None
        for a in range(0, rows, step):
            x = x_ref[0, :, a * rows : (a + step) * rows]
            mix = dot(x, depth_rows, 0, 0).reshape(step, rows, -1)
            if first:
                at = pl.ds(target + a, step)
                out_ref[at, :] += jnp.sum(mix * tile[None], axis=1)
            else:
                term = jnp.sum(mix * tile[a : a + step][:, None, :], axis=0)
                total = term if total is None else total + term
        if not first:
            out_ref[pl.ds(target, rows), :] += total


def mix_pass(first, x, load_id, store_id, depth_id, count, c, f, out_rows):
    cap, rows, width = x.shape
    rank = c.shape[1]
    whole = lambda a: pl.BlockSpec(a.shape, lambda s, *_: (0, 0))
    return pl.pallas_call(
        functools.partial(pass_kernel, first, rows),
        out_shape=jax.ShapeDtypeStruct((out_rows, rank), jnp.float32),
        grid_spec=pltpu.PrefetchScalarGridSpec(
            num_scalar_prefetch=4,
            grid=(cap,),
            in_specs=[
                pl.BlockSpec(
                    (1, rows, width),
                    lambda s, l, t, d, n: (jnp.minimum(s, n[0] - 1), 0, 0),
                ),
                whole(c),
                whole(f),
            ],
            out_specs=pl.BlockSpec((out_rows, rank), lambda s, *_: (0, 0)),
        ),
        cost_estimate=pl.CostEstimate(
            flops=cap * rows * width * rank * 8, bytes_accessed=x.size * 2, transcendentals=0
        ),
        compiler_params=pltpu.CompilerParams(vmem_limit_bytes=40 * 1024 * 1024),
    )(load_id, store_id, depth_id, count, x, c, f)


def root_steps(gram_ref, gram_c_ref, w_ref, work):
    rank = gram_ref.shape[0]
    pair = 2 * NB
    work[:, :rank] = gram_ref[...] * gram_c_ref[...]
    row_id = lax.broadcasted_iota(jnp.int32, (rank, rank), 0)
    col_id = lax.broadcasted_iota(jnp.int32, (rank, rank), 1)
    work[:, rank:] = (row_id == col_id).astype(jnp.float32)
    row = lax.broadcasted_iota(jnp.int32, (NB, pair), 0)
    lane = lax.broadcasted_iota(jnp.int32, (NB, pair), 1)

    for k in range(rank // NB):
        lo, hi = k * NB, (k + 1) * NB
        at = lo // pair * pair
        tile = work[lo:hi, at : at + pair]
        if lo != at:
            tile = pltpu.roll(tile, NB, 1)
        full = jnp.where(lane < NB, tile, (lane - NB == row).astype(jnp.float32))
        parts = []
        for j in range(0, NB, 2):
            inner = j % 8
            if inner == 0 and j > 0:
                parts.append(full[:8])
                full = full[8:]
            first = jnp.broadcast_to(full[:, j : j + 1], full.shape)
            second = jnp.broadcast_to(full[:, j + 1 : j + 2], full.shape)
            row0 = full[inner : inner + 1, :]
            row1 = full[inner + 1 : inner + 2, :]
            p = first[inner : inner + 1, :]
            q = second[inner : inner + 1, :]
            r = second[inner + 1 : inner + 2, :]
            inverse = 1.0 / (p * r - q * q)
            scaled0 = (r * row0 - q * row1) * inverse
            scaled1 = (p * row1 - q * row0) * inverse
            term = first * scaled0 + second * scaled1
            full = full - jnp.where(row[: full.shape[0]] > inner + 1, term, 0.0)
        parts.append(full)
        done = jnp.concatenate(parts, axis=0)
        above = pltpu.roll(done, 1, 0)
        odd = row % 2 == 1
        before = lane == row - 1
        p = jnp.sum(jnp.where(before, above, 0.0), axis=1, keepdims=True)
        q = jnp.sum(jnp.where(before, done, 0.0), axis=1, keepdims=True)
        ratio = q / jnp.where(odd, p, 1.0)
        done = jnp.where(odd, done - ratio * above, done)
        diag = jnp.sum(jnp.where(lane == row, done, 0.0), axis=1, keepdims=True)
        root = (done * lax.rsqrt(diag))[:, NB:]
        stop = rank + (hi + pair - 1) // pair * pair
        w_ref[lo:hi, :] = jnp.zeros((NB, rank), jnp.float32)
        tail = dot(root, work[lo:hi, rank:stop], 1, 0, HIGH)
        w_ref[lo:hi, : stop - rank] = tail
        if hi < rank:
            start = hi // pair * pair
            head = dot(root, work[lo:hi, start:rank], 1, 0, HIGH)
            work[start:rank, start:rank] -= dot(head, head, 0, 0, HIGH)
            work[hi:rank, rank:stop] -= dot(head, tail, 0, 0, HIGH)[hi - start :]


def greet(axes):
    barrier = pltpu.get_barrier_semaphore()
    total = 0
    for axis, n in axes.items():
        me = lax.axis_index(axis)
        for k in range(1, n):
            pl.semaphore_signal(
                barrier, inc=1, device_id={axis: lax.rem(me + k, n)}, device_id_type=pl.DeviceIdType.MESH
            )
        total += n - 1
    pl.semaphore_wait(barrier, total)


def exchange(axis, n, source, target, sems):
    me = lax.axis_index(axis)
    copies = []
    for k in range(1, n):
        peer = lax.rem(me + k, n)
        copy = pltpu.make_async_remote_copy(
            src_ref=source(peer),
            dst_ref=target,
            send_sem=sems.at[0, k - 1],
            recv_sem=sems.at[1, k - 1],
            device_id={axis: peer},
            device_id_type=pl.DeviceIdType.MESH,
        )
        copy.start()
        copies.append(copy)
    return copies


def finish(copies):
    for copy in copies:
        copy.wait()


def added(stage, n):
    total = stage[0]
    for i in range(1, n):
        total = total + stage[i]
    return total


def share(index, rows):
    return pl.ds(pl.multiple_of(index * rows, rows), rows)


def sum_all(wide, narrow, part, out, stage_w, stage_n, sems_w, sems_n, sems_g, beside=None):
    me_w, me_n = lax.axis_index("wide"), lax.axis_index("narrow")
    rows = part.shape[0] // wide
    mine = share(me_w, rows)
    copies = exchange("wide", wide, lambda peer: part.at[share(peer, rows)], stage_w.at[me_w], sems_w)
    stage_w[me_w] = part[mine, :]
    if beside is not None:
        beside()
    finish(copies)
    stage_n[me_n] = added(stage_w, wide)
    finish(exchange("narrow", narrow, lambda peer: stage_n.at[me_n], stage_n.at[me_n], sems_n))
    out[mine, :] = added(stage_n, narrow)
    finish(exchange("wide", wide, lambda peer: out.at[mine], out.at[mine], sems_g))


def sum_scratch(wide, narrow, rank):
    return [
        pltpu.VMEM((rank, rank), jnp.float32),
        pltpu.VMEM((wide, rank // wide, rank), jnp.float32),
        pltpu.VMEM((narrow, rank // wide, rank), jnp.float32),
        pltpu.SemaphoreType.DMA((2, wide)),
        pltpu.SemaphoreType.DMA((2, narrow)),
        pltpu.SemaphoreType.DMA((2, wide)),
    ]


def params(collective):
    return pltpu.CompilerParams(
        collective_id=collective, has_side_effects=True, vmem_limit_bytes=40 * 1024 * 1024
    )


def start_kernel(wide, narrow, b_ref, c_ref, rows_ref, gram_ref, gram_c_ref, part, *rest):
    *sum_rest, sems = rest
    me = lax.axis_index("wide")
    rows = b_ref.shape[0]
    greet({"wide": wide, "narrow": narrow})
    b = b_ref[...]
    part[...] = dot(b, b, 0, 0)
    mine = share(me, rows)

    def beside():
        rows_ref[mine, :] = b
        c = c_ref[...]
        gram_c_ref[...] = dot(c, c, 0, 0)

    copies = exchange("wide", wide, lambda peer: b_ref, rows_ref.at[mine], sems)
    sum_all(wide, narrow, part, gram_ref, *sum_rest, beside)
    finish(copies)


def start(wide, narrow, b, c):
    rows, rank = b.shape
    return pl.pallas_call(
        functools.partial(start_kernel, wide, narrow),
        out_shape=[
            jax.ShapeDtypeStruct((wide * rows, rank), b.dtype),
            jax.ShapeDtypeStruct((rank, rank), jnp.float32),
            jax.ShapeDtypeStruct((rank, rank), jnp.float32),
        ],
        in_specs=[VMEM] * 2,
        out_specs=[VMEM] * 3,
        scratch_shapes=sum_scratch(wide, narrow, rank) + [pltpu.SemaphoreType.DMA((2, wide))],
        compiler_params=params(0),
    )(b, c)


def middle_kernel(wide, narrow, sum_ref, gram_b_ref, gram_c_ref, new_ref, rows_ref, gram_ref, part, *rest):
    *sum_rest, stage, sems, sems_a, w_ref, work = rest
    me = lax.axis_index("narrow")
    rows = new_ref.shape[0]
    greet({"wide": wide, "narrow": narrow})
    mine = share(me, rows)
    copies = exchange("narrow", narrow, lambda peer: sum_ref.at[share(peer, rows)], stage.at[me], sems)
    stage[me] = sum_ref[mine, :]
    root_steps(gram_b_ref, gram_c_ref, w_ref, work)
    finish(copies)
    w = w_ref[...]
    new = dot(dot(added(stage, narrow), w, 1, 1, HIGH), w, 1, 0, HIGH)
    half = new.astype(jnp.bfloat16)
    rows_ref[mine, :] = half
    copies = exchange("narrow", narrow, lambda peer: rows_ref.at[mine], rows_ref.at[mine], sems_a)
    part[...] = dot(half, half, 0, 0)

    def beside():
        new_ref[...] = new

    sum_all(wide, narrow, part, gram_ref, *sum_rest, beside)
    finish(copies)


def middle(wide, narrow, first_part, gram_b, gram_c):
    rows, rank = first_part.shape[0] // narrow, first_part.shape[1]
    return pl.pallas_call(
        functools.partial(middle_kernel, wide, narrow),
        out_shape=[
            jax.ShapeDtypeStruct((rows, rank), jnp.float32),
            jax.ShapeDtypeStruct((narrow * rows, rank), jnp.bfloat16),
            jax.ShapeDtypeStruct((rank, rank), jnp.float32),
        ],
        in_specs=[VMEM] * 3,
        out_specs=[VMEM] * 3,
        scratch_shapes=sum_scratch(wide, narrow, rank)
        + [
            pltpu.VMEM((narrow, rows, rank), jnp.float32),
            pltpu.SemaphoreType.DMA((2, narrow)),
            pltpu.SemaphoreType.DMA((2, narrow)),
            pltpu.VMEM((rank, rank), jnp.float32),
            pltpu.VMEM((rank, 2 * rank), jnp.float32),
        ],
        compiler_params=params(1),
    )(first_part, gram_b, gram_c)


def last_kernel(wide, sum_ref, gram_a_ref, gram_c_ref, new_ref, stage, sems, w_ref, work):
    me = lax.axis_index("wide")
    rows = new_ref.shape[0]
    greet({"wide": wide})
    copies = exchange("wide", wide, lambda peer: sum_ref.at[share(peer, rows)], stage.at[me], sems)
    stage[me] = sum_ref[share(me, rows), :]
    root_steps(gram_a_ref, gram_c_ref, w_ref, work)
    finish(copies)
    w = w_ref[...]
    new_ref[...] = dot(dot(added(stage, wide), w, 1, 1, HIGH), w, 1, 0, HIGH)


def last(wide, second_part, gram_a, gram_c):
    rows, rank = second_part.shape[0] // wide, second_part.shape[1]
    return pl.pallas_call(
        functools.partial(last_kernel, wide),
        out_shape=jax.ShapeDtypeStruct((rows, rank), jnp.float32),
        in_specs=[VMEM] * 3,
        out_specs=VMEM,
        scratch_shapes=[
            pltpu.VMEM((wide, rows, rank), jnp.float32),
            pltpu.SemaphoreType.DMA((2, wide)),
            pltpu.VMEM((rank, rank), jnp.float32),
            pltpu.VMEM((rank, 2 * rank), jnp.float32),
        ],
        compiler_params=params(2),
    )(second_part, gram_a, gram_c)


def local(blocks, row_tile, col_tile, depth_tile, block_count, factor_b, factor_c):
    x = blocks[0, 0]
    first_ids = row_tile[0, 0]
    second_ids = col_tile[0, 0]
    depth_ids = depth_tile[0, 0]
    count = block_count[0]
    wide = lax.axis_size("wide")
    narrow = lax.axis_size("narrow")
    rows = factor_b.shape[0]

    b_rows, gram_b, gram_c = start(wide, narrow, factor_b, factor_c)
    first_part = mix_pass(
        True, x, second_ids, first_ids, depth_ids, count, factor_c, b_rows, narrow * rows
    )
    a_new, a_rows, gram_a = middle(wide, narrow, first_part, gram_b, gram_c)
    second_part = mix_pass(
        False, x, first_ids, second_ids, depth_ids, count, factor_c, a_rows, wide * rows
    )
    b_new = last(wide, second_part, gram_a, gram_c)
    return (a_new, b_new)


def solution(mesh):
    return jax.shard_map(
        local,
        mesh=mesh,
        in_specs=(
            P("wide", "narrow", None, None, None),
            P("wide", "narrow", None),
            P("wide", "narrow", None),
            P("wide", "narrow", None),
            P("wide", "narrow"),
            P(("wide", "narrow"), None),
            P(),
        ),
        out_specs=(P(("wide", "narrow"), None), P(("wide", "narrow"), None)),
        check_vma=False,
    )
```
